32 devices in a mesh: groups: 2 (over x), cross: 8 (over z, y), node: 2 (over core).
Axes of the slice: x: 2, y: 2, z: 4, core: 2. Of those that a mesh axis runs over, the one named last changes fastest.
Arguments:
- tokens: bfloat16 [4096, 2560], P(('groups', 'cross', 'node')), parts along dimension 0, may hold values from -0.59765625 to 0.59765625
- grad_out: bfloat16 [4096, 2560], P(('groups', 'cross', 'node')), parts along dimension 0, may hold values from -6 to 6
- expert_ids: int32 [4096, 1], P(('groups', 'cross', 'node')), parts along dimension 0, may hold values from 0 to 1; in each aligned block of 128 rows (0 to 127, 128 to 255, ...) at most 72 rows name the same one
- routed_pre: bfloat16 [2, 4608, 4096], P(None, ('groups', 'node'), 'cross'), parts along dimension 1, may hold values from -6 to 6
- shared_pre: bfloat16 [2, 4608, 4096], P(None, ('groups', 'node'), 'cross'), parts along dimension 1, may hold values from -6 to 6
- w_gate: bfloat16 [2, 2560, 4096], P('node', None, 'cross'), may hold values from -0.125 to 0.125
- w_up: bfloat16 [2, 2560, 4096], P('node', None, 'cross'), may hold values from -0.125 to 0.125
- w_down: bfloat16 [2, 4096, 2560], P('node', 'cross'), may hold values from -0.09375 to 0.09375
- s_gate: bfloat16 [2560, 4096], P(None, 'cross'), may hold values from -0.125 to 0.125
- s_up: bfloat16 [2560, 4096], P(None, 'cross'), may hold values from -0.125 to 0.125
- s_down: bfloat16 [4096, 2560], P('cross'), may hold values from -0.09375 to 0.09375
Outputs:
- grad_tokens: bfloat16 [4096, 2560], P(('groups', 'cross', 'node')), parts along dimension 0
- grad_shared_gate: float32 [5120, 4096], P(('groups', 'node'), 'cross'), parts along dimension 0
- grad_shared_up: float32 [5120, 4096], P(('groups', 'node'), 'cross'), parts along dimension 0
- grad_shared_down: float32 [8192, 2560], P(('groups', 'cross'), 'node'), parts along dimension 0
The draws below stay inside these ranges and needn't reach their ends.
There are 2 independent parts, one for each index of `groups`. The reference program is written for one: setup_inputs(seed, part) draws one part's arguments, and reference() takes and returns one part's arrays. A program takes and returns all parts, laid end to end along the dimension named above; an argument that names none is the same for every part. Nothing has to cross between parts.
Inputs may be any that keep to these rules, and one draw needn't show every extreme that they name: `expert_ids`: within the tokens of one device (aligned blocks of 128 rows) no expert is named more than 72 times, and in every draw some block names some expert exactly 72 times. Rows of routed_pre and shared_pre whose slot holds no token are read by no output.
All inputs are finite; a program needn't handle non-finite values.
Results may differ from the reference program's by a relative error of at most 0.012.
Values may be sent and summed in bfloat16 or wider, within the bound.
A program may use at most 256 MiB of HBM per device.

```python
import math
import jax
import jax.numpy as jnp
import numpy as np
from jax import lax

D = 2560
FF = 4096
SH = 4096
TOK_DEV = 128
CAP = 72
EXPERTS = 2
TOKENS = 2048
ROWS = 1152
N_CROSS = 8
N_NODE = 2


def shard_levels(key, shape, cuts, low, high):
    factor_of, own = 1.0, jax.random.fold_in(key, 6)
    for position, parts in cuts:
        draws = jnp.exp(jax.random.uniform(jax.random.fold_in(own, position), (parts,), jnp.float32, low / len(cuts), high / len(cuts)))
        factor_of = factor_of * jnp.repeat(draws, shape[position] // parts).reshape([-1 if axis == position else 1 for axis in range(len(shape))])
    return factor_of


def assign_block(key, own, number, rows, count, top, bound, skew):
    sequence = jax.random.permutation(key, count)
    crowded, ordinary = load_shares(count, rows * top, bound, skew, True), load_shares(count, rows * top, bound, skew, False)
    places = jnp.arange(count)

    def named(lengths, offset_by):
        used = int((lengths > 0).sum())
        fixed = max(1, used // 4)
        shifted = fixed + (places - fixed + offset_by * (used - fixed)) % max(1, count - fixed)
        return jnp.zeros((count,), jnp.int32).at[sequence[jnp.where(places < fixed, places, shifted)]].set(jnp.asarray(lengths, jnp.int32))

    lengths = jnp.where(number % 4 == 0, named(crowded, number // 4), named(ordinary, number - number // 4 - 1))
    mixed = jax.random.permutation(jax.random.fold_in(own, 3), count)
    giver, receiver = mixed[0:count // 2 * 2:2], mixed[1:count // 2 * 2:2]
    margin = jnp.minimum(lengths[giver] - 1, bound - lengths[receiver]) // 2
    margin = jnp.where((giver == sequence[0]) | (receiver == sequence[0]) | (lengths[receiver] == 0), 0, jnp.maximum(margin, 0))
    shifted = jax.random.randint(jax.random.fold_in(own, 4), (count // 2,), 0, 1 << 20) % (margin + 1)
    lengths = lengths.at[giver].add(-shifted).at[receiver].add(shifted)
    labels = jnp.searchsorted(jnp.cumsum(lengths), jnp.arange(rows * top), side="right").astype(jnp.int32)
    listing = labels.reshape(top, rows).T
    listing = listing[jax.random.permutation(jax.random.fold_in(own, 1), rows)]
    offset_by = jax.random.randint(jax.random.fold_in(own, 2), (rows, 1), 0, top)
    return jnp.take_along_axis(listing, (jnp.arange(top)[None, :] + offset_by) % top, axis=1)


def load_shares(number_of, total, bound, slope, full):
    portions = [(1 << 20) // math.isqrt(grade ** slope) + 1 for grade in range(1, number_of + 1)]
    largest = bound if full else min(bound, max(-(-total // number_of), total * portions[0] // sum(portions)))
    least = 1 if total - largest >= number_of - 1 else 0
    given, spare = [largest] + [least] * (number_of - 1), total - largest - least * (number_of - 1)
    while spare > 0:
        movable = [i for i in range(1, number_of) if given[i] < largest] or [i for i in range(1, number_of) if given[i] < bound]
        mass, remaining = sum([portions[i] for i in movable]), spare
        for i in movable:
            more = min(bound - given[i], max(1, remaining * portions[i] // mass), spare)
            given[i] = given[i] + more
            spare = spare - more
    return np.array(given)


def normal_values(key, extent, spread, most, shards=(), held_as=jnp.bfloat16):
    loudness = shard_levels(key, extent, shards, -0.22, 0.18) if shards else 1.0
    array = jax.random.normal(key, extent, jnp.float32) * spread * loudness
    return jnp.minimum(jnp.maximum(array, -most), most).astype(held_as)


def setup_inputs(seed: int = 0, part: int = 0) -> dict:
    key_list = jax.random.split(jax.random.key(seed), 12)
    part_splits = jax.random.split(jax.random.fold_in(key_list[11], part), 12)
    tokens = normal_values(part_splits[0], (TOKENS, D), 0.1, 0.59765625, ((0, 16),))
    grad_out = normal_values(part_splits[1], (TOKENS, D), 1.0, 6.0, ((0, 16),))
    expert_ids_keys = jax.random.split(jax.random.fold_in(part_splits[2], 1), TOKENS // TOK_DEV)
    expert_ids_turns = jax.random.permutation(jax.random.fold_in(part_splits[2], 3), TOKENS // TOK_DEV)
    expert_ids = jax.vmap(lambda own, number: assign_block(jax.random.fold_in(part_splits[2], 2), own, number, TOK_DEV, EXPERTS, 1, CAP, 2))(expert_ids_keys, expert_ids_turns).reshape((TOKENS, 1))
    routed_pre = normal_values(part_splits[3], (2, EXPERTS * ROWS, FF), 1.0, 6.0, ((1, 2), (2, 8)))
    shared_pre = normal_values(part_splits[4], (2, EXPERTS * ROWS, SH), 1.0, 6.0, ((1, 2), (2, 8)))
    w_gate = normal_values(key_list[5], (EXPERTS, D, FF), D ** -0.5, 0.125, ((0, 2), (2, 8)))
    w_up = normal_values(key_list[6], (EXPERTS, D, FF), D ** -0.5, 0.125, ((0, 2), (2, 8)))
    w_down = normal_values(key_list[7], (EXPERTS, FF, D), FF ** -0.5, 0.09375, ((0, 2), (1, 8)))
    s_gate = normal_values(key_list[8], (D, SH), D ** -0.5, 0.125, ((1, 8),))
    s_up = normal_values(key_list[9], (D, SH), D ** -0.5, 0.125, ((1, 8),))
    s_down = normal_values(key_list[10], (SH, D), SH ** -0.5, 0.09375, ((0, 8),))
    return dict(tokens=tokens, grad_out=grad_out, expert_ids=expert_ids, routed_pre=routed_pre, shared_pre=shared_pre, w_gate=w_gate, w_up=w_up, w_down=w_down, s_gate=s_gate, s_up=s_up, s_down=s_down)


def silu_parts(pre_gate, pre_up, grad_hidden):
    sigma = jax.nn.sigmoid(pre_gate)
    active = pre_gate * sigma
    d_gate = grad_hidden * pre_up * sigma * (1.0 + pre_gate * (1.0 - sigma))
    d_up = grad_hidden * active
    return d_gate, d_up, active * pre_up


def right_t(left, right):
    return lax.dot_general(left, right, (((1,), (1,)), ((), ())), preferred_element_type=jnp.float32)


def left_t(left, right):
    return lax.dot_general(left, right, (((0,), (0,)), ((), ())), preferred_element_type=jnp.float32)


def reference(tokens, grad_out, expert_ids, routed_pre, shared_pre, w_gate, w_up, w_down, s_gate, s_up, s_down):
    blocks = N_CROSS * N_NODE
    rows_all = blocks * CAP
    ids = expert_ids[:, 0]
    onehot = (ids[:, None] == jnp.arange(EXPERTS, dtype=jnp.int32)[None, :]).astype(jnp.int32)
    ranks = jnp.cumsum(onehot.reshape(blocks, TOK_DEV, EXPERTS), axis=1).reshape(TOKENS, EXPERTS) - 1
    slot_of = jnp.sum(ranks * onehot, axis=1).astype(jnp.int32)
    row_index = ((jnp.arange(TOKENS, dtype=jnp.int32) // TOK_DEV) * CAP + slot_of).astype(jnp.int32)
    grad_rows = jnp.zeros((EXPERTS, rows_all, D), jnp.bfloat16).at[ids, row_index].set(grad_out)
    token_rows = jnp.zeros((EXPERTS, rows_all, D), jnp.bfloat16).at[ids, row_index].set(tokens)
    hidden_step = FF // N_CROSS
    shared_step = SH // N_CROSS
    per_expert = []
    total_gate = jnp.zeros((D, SH), jnp.float32)
    total_up = jnp.zeros((D, SH), jnp.float32)
    total_down = jnp.zeros((SH, D), jnp.float32)
    for expert in range(EXPERTS):
        dy_rows = grad_rows[expert]
        x_rows = token_rows[expert]
        routed = routed_pre[:, expert * rows_all:(expert + 1) * rows_all]
        shared = shared_pre[:, expert * rows_all:(expert + 1) * rows_all]
        gate_w = w_gate[expert]
        up_w = w_up[expert]
        down_w = w_down[expert]

        def block(carry, index):
            start = (index * hidden_step).astype(jnp.int32)
            sstart = (index * shared_step).astype(jnp.int32)
            gate_k = lax.dynamic_slice_in_dim(gate_w, start, hidden_step, 1)
            up_k = lax.dynamic_slice_in_dim(up_w, start, hidden_step, 1)
            down_k = lax.dynamic_slice_in_dim(down_w, start, hidden_step, 0)
            pre_g = lax.dynamic_slice_in_dim(routed[0], start, hidden_step, 1).astype(jnp.float32)
            pre_u = lax.dynamic_slice_in_dim(routed[1], start, hidden_step, 1).astype(jnp.float32)
            sgate_k = lax.dynamic_slice_in_dim(s_gate, sstart, shared_step, 1)
            sup_k = lax.dynamic_slice_in_dim(s_up, sstart, shared_step, 1)
            sdown_k = lax.dynamic_slice_in_dim(s_down, sstart, shared_step, 0)
            spre_g = lax.dynamic_slice_in_dim(shared[0], sstart, shared_step, 1).astype(jnp.float32)
            spre_u = lax.dynamic_slice_in_dim(shared[1], sstart, shared_step, 1).astype(jnp.float32)
            d_gate, d_up, unused = silu_parts(pre_g, pre_u, right_t(dy_rows, down_k))
            sh_gate, sh_up, shared_act = silu_parts(spre_g, spre_u, right_t(dy_rows, sdown_k))
            d_gate = d_gate.astype(jnp.bfloat16)
            d_up = d_up.astype(jnp.bfloat16)
            sh_gate = sh_gate.astype(jnp.bfloat16)
            sh_up = sh_up.astype(jnp.bfloat16)
            shared_act = shared_act.astype(jnp.bfloat16)
            part = right_t(d_gate, gate_k) + right_t(d_up, up_k) + right_t(sh_gate, sgate_k) + right_t(sh_up, sup_k)
            part = lax.optimization_barrier(part.astype(jnp.bfloat16)).astype(jnp.float32)
            grads = (left_t(x_rows, sh_gate), left_t(x_rows, sh_up), left_t(shared_act, dy_rows))
            return carry + part, grads

        summed, grads = lax.scan(block, jnp.zeros((rows_all, D), jnp.float32), jnp.arange(N_CROSS, dtype=jnp.int32))
        per_expert.append(summed.astype(jnp.bfloat16))
        total_gate = total_gate + grads[0].transpose(1, 0, 2).reshape(D, SH)
        total_up = total_up + grads[1].transpose(1, 0, 2).reshape(D, SH)
        total_down = total_down + grads[2].reshape(SH, D)
    grad_rows_in = jnp.stack(per_expert)
    grad_tokens = grad_rows_in[ids, row_index]
    return grad_tokens, total_gate, total_up, total_down
```

```python
import functools

import jax
import jax.numpy as jnp
from jax import lax
from jax.experimental import pallas as pl
from jax.experimental.pallas import tpu as pltpu
from jax.sharding import PartitionSpec as P

CAP = 72
MESH = pl.DeviceIdType.MESH
GATHER_PIECES = 2
REDUCE_PIECES = 3


def silu_parts(pre_gate, pre_up, grad_hidden):
    sigma = jax.nn.sigmoid(pre_gate)
    active = pre_gate * sigma
    d_gate = grad_hidden * pre_up * sigma * (1.0 + pre_gate * (1.0 - sigma))
    d_up = grad_hidden * active
    return (d_gate, d_up, active * pre_up)


def right_t(left, right):
    return lax.dot_general(
        left, right, (((1,), (1,)), ((), ())), preferred_element_type=jnp.float32
    )


def left_t(left, right):
    return lax.dot_general(
        left, right, (((0,), (0,)), ((), ())), preferred_element_type=jnp.float32
    )


def place(depth):
    cross = lax.axis_index("cross")
    return lax.div(cross, 2), lax.rem(cross, 2), lax.axis_index("node")


def greet(z, y, n, depth):
    barrier = pltpu.get_barrier_semaphore()

    def tell(zz, yy, nn):
        pl.semaphore_signal(
            barrier, inc=1, device_id={"cross": zz * 2 + yy, "node": nn}, device_id_type=MESH
        )

    tell(z, 1 - y, n)
    tell(z, y, 1 - n)

    @pl.when(z < depth - 1)
    def _():
        tell(z + 1, y, n)

    @pl.when(z > 0)
    def _():
        tell(z - 1, y, n)

    count = 2 + (z < depth - 1).astype(jnp.int32) + (z > 0).astype(jnp.int32)
    pl.semaphore_wait(barrier, count)


def gather_kernel(
    depth, dy, ids, x, dy_all, ids_all, xh,
    recv, recv_b, send_r, send_l, send_y, send_b, x_send, x_recv, local_sem,
):
    z, y, n = place(depth)
    rows = dy.shape[0] // GATHER_PIECES
    half = xh.shape[-1]
    pieces = GATHER_PIECES + 1
    greet(z, y, n, depth)

    def slot(c, core, h):
        if h < GATHER_PIECES:
            return dy_all.at[c, core, pl.ds(h * rows, rows)]
        return ids_all.at[c, core]

    def own(h):
        if h < GATHER_PIECES:
            return dy.at[pl.ds(h * rows, rows)]
        return ids

    def copy(src, c, h, send_sem, recv_sem, zz, yy, nn):
        return pltpu.make_async_remote_copy(
            src_ref=src,
            dst_ref=slot(c, n, h),
            send_sem=send_sem,
            recv_sem=recv_sem.at[c, h],
            device_id={"cross": zz * 2 + yy, "node": nn},
            device_id_type=MESH,
        )

    def right(src, zb, h):
        return copy(src, zb * 2 + y, h, send_r.at[zb, h], recv, z + 1, y, n)

    def left(src, zb, h):
        return copy(src, zb * 2 + y, h, send_l.at[zb, h], recv, z - 1, y, n)

    def across(src, zb, h):
        return copy(src, zb * 2 + y, h, send_y.at[zb, h], recv, z, 1 - y, n)

    def sibling(src, c, h):
        return copy(src, c, h, send_b.at[c, h], recv_b, z, y, 1 - n)

    def arrived(c, h):
        pltpu.make_async_remote_copy(
            src_ref=slot(c, n, h), dst_ref=slot(c, n, h), send_sem=send_b.at[c, h],
            recv_sem=recv.at[c, h], device_id={"cross": z * 2 + y, "node": 1 - n},
            device_id_type=MESH,
        ).wait_recv()

    def arrived_b(c, h):
        pltpu.make_async_remote_copy(
            src_ref=slot(c, 1 - n, h), dst_ref=slot(c, 1 - n, h), send_sem=send_b.at[c, h],
            recv_sem=recv_b.at[c, h], device_id={"cross": z * 2 + y, "node": 1 - n},
            device_id_type=MESH,
        ).wait_recv()

    def mine(src, zb, h, act):
        @pl.when((z < depth - 1) & (zb <= z))
        def _():
            act(right(src, zb, h))

        @pl.when((z > 0) & (zb >= z))
        def _():
            act(left(src, zb, h))

        act(across(src, zb, h))
        act(sibling(src, zb * 2 + y, h))

    def start(d):
        d.start()

    def done(d):
        d.wait_send()

    def walk(s, act):
        if s == 0:
            act(z)
        else:
            @pl.when(z - s >= 0)
            def _():
                act(z - s)

            @pl.when(z + s < depth)
            def _():
                act(z + s)

    order = [GATHER_PIECES] + list(range(GATHER_PIECES))
    for h in order:
        mine(own(h), z, h, start)
    keep = pl.multiple_of(n * half, 128)
    give = pl.multiple_of((1 - n) * half, 128)
    x_out = pltpu.make_async_remote_copy(
        src_ref=x.at[:, pl.ds(give, half)], dst_ref=xh.at[n], send_sem=x_send, recv_sem=x_recv,
        device_id={"cross": z * 2 + y, "node": 1 - n}, device_id_type=MESH,
    )
    x_out.start()
    locals_ = [
        pltpu.make_async_copy(dy, dy_all.at[z * 2 + y, n], local_sem.at[0]),
        pltpu.make_async_copy(ids, ids_all.at[z * 2 + y, n], local_sem.at[1]),
        pltpu.make_async_copy(x.at[:, pl.ds(keep, half)], xh.at[n], local_sem.at[2]),
    ]
    for d in locals_:
        d.start()

    def down(h):
        def act(zb):
            arrived(zb * 2 + y, h)
            mine(slot(zb * 2 + y, n, h), zb, h, start)
        return act

    def over(h):
        def act(zb):
            c = zb * 2 + 1 - y
            arrived(c, h)
            sibling(slot(c, n, h), c, h).start()
        return act

    for s in range(1, depth + 1):
        for h in order:
            if s < depth:
                walk(s, down(h))
            walk(s - 1, over(h))

    for d in locals_:
        d.wait()
    x_out.wait_send()
    pltpu.make_async_remote_copy(
        src_ref=xh.at[1 - n], dst_ref=xh.at[1 - n], send_sem=x_send, recv_sem=x_recv,
        device_id={"cross": z * 2 + y, "node": 1 - n}, device_id_type=MESH,
    ).wait_recv()
    for h in range(pieces):
        for zb in range(depth):
            mine(slot(zb * 2 + y, n, h), zb, h, done)
            c = zb * 2 + 1 - y
            sibling(slot(c, n, h), c, h).wait_send()
            arrived_b(zb * 2, h)
            arrived_b(zb * 2 + 1, h)


def gather(dy, ids, x, count):
    depth = count // 2
    rows, width = dy.shape
    pieces = GATHER_PIECES + 1
    dma = pltpu.SemaphoreType.DMA
    hbm = pl.BlockSpec(memory_space=pl.ANY)
    return pl.pallas_call(
        functools.partial(gather_kernel, depth),
        out_shape=(
            jax.ShapeDtypeStruct((count, 2, rows, width), dy.dtype),
            jax.ShapeDtypeStruct((count, 2) + ids.shape, ids.dtype),
            jax.ShapeDtypeStruct((2, rows, width // 2), x.dtype),
        ),
        in_specs=[hbm] * 3,
        out_specs=(hbm,) * 3,
        scratch_shapes=[
            dma((count, pieces)),
            dma((count, pieces)),
            dma((depth, pieces)),
            dma((depth, pieces)),
            dma((depth, pieces)),
            dma((count, pieces)),
            dma,
            dma,
            dma((3,)),
        ],
        compiler_params=pltpu.CompilerParams(collective_id=0, has_side_effects=True),
        name="gather_rows",
    )(dy, ids, x)


def reduce_kernel(
    depth, part, out, y_buf, r_buf, l_buf, held,
    y_send, y_recv, r_send, r_recv, l_send, l_recv, b_send, b_recv,
):
    z, y, n = place(depth)
    rows = part.shape[2] // REDUCE_PIECES
    greet(z, y, n, depth)

    def at(ref, d, h):
        return ref.at[d, pl.ds(h * rows, rows)]

    def copy(src, dst, send_sem, recv_sem, zz, yy, nn):
        return pltpu.make_async_remote_copy(
            src_ref=src, dst_ref=dst, send_sem=send_sem, recv_sem=recv_sem,
            device_id={"cross": zz * 2 + yy, "node": nn}, device_id_type=MESH,
        )

    def across(d, h):
        return copy(
            part.at[d, 1 - y, pl.ds(h * rows, rows)], at(y_buf, d, h),
            y_send.at[d, h], y_recv.at[d, h], z, 1 - y, n,
        )

    def right(d, h):
        return copy(
            at(held, d, h), at(r_buf, d, h), r_send.at[d, h], r_recv.at[d, h], z + 1, y, n
        )

    def left(d, h):
        return copy(
            at(held, d, h), at(l_buf, d, h), l_send.at[d, h], l_recv.at[d, h], z - 1, y, n
        )

    def sibling(h):
        return copy(
            at(out, n, h), at(out, n, h), b_send.at[h], b_recv.at[h], z, y, 1 - n
        )

    def walk(s, act):
        if s == 0:
            act(z)
        else:
            @pl.when(z + s < depth)
            def _():
                act(z + s)

            @pl.when(z - s >= 0)
            def _():
                act(z - s)

    def begin(s):
        for h in range(REDUCE_PIECES):
            walk(s, lambda d, h=h: across(d, h).start())

    def base(d, h):
        across(d, h).wait_recv()
        return part[d, y, pl.ds(h * rows, rows)].astype(jnp.float32) + y_buf[
            d, pl.ds(h * rows, rows)
        ].astype(jnp.float32)

    begin(depth - 1)
    for s in range(depth - 1, 0, -1):
        begin(s - 1)
        for h in range(REDUCE_PIECES):
            span = pl.ds(h * rows, rows)

            @pl.when(z + s < depth)
            def _():
                d = z + s
                value = base(d, h)
                if s == depth - 1:
                    held[d, span] = value.astype(held.dtype)
                else:
                    @pl.when(z == 0)
                    def _():
                        held[d, span] = value.astype(held.dtype)

                    @pl.when(z > 0)
                    def _():
                        right(d, h).wait_recv()
                        total = value + r_buf[d, span].astype(jnp.float32)
                        held[d, span] = total.astype(held.dtype)

                right(d, h).start()

            @pl.when(z - s >= 0)
            def _():
                d = z - s
                value = base(d, h)
                if s == depth - 1:
                    held[d, span] = value.astype(held.dtype)
                else:
                    @pl.when(z == depth - 1)
                    def _():
                        held[d, span] = value.astype(held.dtype)

                    @pl.when(z < depth - 1)
                    def _():
                        left(d, h).wait_recv()
                        total = value + l_buf[d, span].astype(jnp.float32)
                        held[d, span] = total.astype(held.dtype)

                left(d, h).start()

    for h in range(REDUCE_PIECES):
        span = pl.ds(h * rows, rows)
        value = base(z, h)

        @pl.when(z == 0)
        def _():
            left(z, h).wait_recv()
            out[n, span] = (value + l_buf[z, span].astype(jnp.float32)).astype(out.dtype)

        @pl.when(z == depth - 1)
        def _():
            right(z, h).wait_recv()
            out[n, span] = (value + r_buf[z, span].astype(jnp.float32)).astype(out.dtype)

        @pl.when((z > 0) & (z < depth - 1))
        def _():
            left(z, h).wait_recv()
            right(z, h).wait_recv()
            total = (
                value + l_buf[z, span].astype(jnp.float32) + r_buf[z, span].astype(jnp.float32)
            )
            out[n, span] = total.astype(out.dtype)

        sibling(h).start()

    for h in range(REDUCE_PIECES):
        for d in range(depth):
            across(d, h).wait_send()

            @pl.when(z < d)
            def _():
                right(d, h).wait_send()

            @pl.when(z > d)
            def _():
                left(d, h).wait_send()

        sibling(h).wait_send()
        copy(
            at(out, 1 - n, h), at(out, 1 - n, h), b_send.at[h], b_recv.at[h], z, y, 1 - n
        ).wait_recv()


def reduce_rows(part, count):
    depth = count // 2
    _, _, rows, width = part.shape
    dma = pltpu.SemaphoreType.DMA
    vmem = pl.BlockSpec(memory_space=pltpu.VMEM)
    pair = (depth, REDUCE_PIECES)
    block = pltpu.VMEM((depth, rows, width), part.dtype)
    return pl.pallas_call(
        functools.partial(reduce_kernel, depth),
        out_shape=jax.ShapeDtypeStruct((2, rows, width), part.dtype),
        in_specs=[vmem],
        out_specs=vmem,
        scratch_shapes=[block] * 4
        + [dma(pair)] * 6
        + [dma((REDUCE_PIECES,))] * 2,
        compiler_params=pltpu.CompilerParams(
            collective_id=1, has_side_effects=True, vmem_limit_bytes=56 * 1024 * 1024
        ),
        name="reduce_rows",
    )(part)


def slots_of(ids, expert):
    named = (ids == expert).astype(jnp.bfloat16)
    tokens = ids.shape[1]
    upper = (
        jnp.arange(tokens)[:, None] <= jnp.arange(tokens)[None, :]
    ).astype(jnp.bfloat16)
    rank = lax.dot_general(
        named, upper, (((1,), (0,)), ((), ())), preferred_element_type=jnp.float32
    ).astype(jnp.int32) - 1
    slot = jnp.where(ids == expert, rank, -1)
    return (slot[:, None, :] == jnp.arange(CAP, dtype=jnp.int32)[None, :, None]).astype(
        jnp.bfloat16
    )


def body(
    tokens, grad_out, expert_ids, routed_pre, shared_pre, w_gate, w_up, w_down, s_gate, s_up, s_down
):
    count = lax.axis_size("cross")
    node = lax.axis_index("node")
    cross = lax.axis_index("cross")
    rows, width = tokens.shape
    half = width // 2
    ids_tile = jnp.broadcast_to(expert_ids[:, 0][None, :], (8, rows))
    dy_all, ids_all, x_half = gather(grad_out, ids_tile, tokens, count)
    x_all = lax.all_gather(x_half.reshape(2 * rows, half), "cross", axis=0, tiled=True)
    blocks = 2 * count
    dy_all = dy_all.reshape(blocks, rows, width)
    ids = ids_all[:, :, 0, :].reshape(blocks, rows)
    to_slots = slots_of(ids, node)
    to_slots_b = slots_of(ids, 1 - node)
    dy_rows = (
        jnp.einsum("bst,btd->bsd", to_slots, dy_all, preferred_element_type=jnp.float32)
        .astype(jnp.bfloat16)
        .reshape(blocks * CAP, width)
    )
    sh_gate, sh_up, shared_act = silu_parts(
        shared_pre[0].astype(jnp.float32),
        shared_pre[1].astype(jnp.float32),
        right_t(dy_rows, s_down),
    )
    sh_gate = sh_gate.astype(jnp.bfloat16)
    sh_up = sh_up.astype(jnp.bfloat16)
    shared_act = shared_act.astype(jnp.bfloat16)
    mine = jnp.concatenate([sh_gate, sh_up, shared_act], axis=1)
    other = lax.ppermute(mine, "node", [(0, 1), (1, 0)])
    d_gate, d_up, _ = silu_parts(
        routed_pre[0].astype(jnp.float32),
        routed_pre[1].astype(jnp.float32),
        right_t(dy_rows, w_down[0]),
    )
    d_gate = d_gate.astype(jnp.bfloat16)
    d_up = d_up.astype(jnp.bfloat16)
    partial_in = (
        right_t(d_gate, w_gate[0])
        + right_t(d_up, w_up[0])
        + right_t(sh_gate, s_gate)
        + right_t(sh_up, s_up)
    ).astype(jnp.bfloat16)
    returned = reduce_rows(partial_in.reshape(count // 2, 2, 2 * CAP, width), count)

    own_ids = expert_ids[:, 0].reshape(1, rows)
    picks = jnp.stack([slots_of(own_ids, e)[0] for e in range(2)])
    picks = jnp.where(
        (jnp.arange(2) == node)[None, :, None, None], picks[:, None], jnp.zeros((), jnp.bfloat16)
    ).reshape(4 * CAP, rows)
    grad_tokens = left_t(picks, returned.reshape(4 * CAP, width)).astype(jnp.bfloat16)

    hidden = mine.shape[1]

    def to_tokens(one_hot, values):
        return jnp.einsum(
            "bst,bsf->btf", one_hot, values.reshape(blocks, CAP, hidden),
            preferred_element_type=jnp.float32,
        )

    by_token = (
        (to_tokens(to_slots, mine) + to_tokens(to_slots_b, other))
        .astype(jnp.bfloat16)
        .reshape(blocks * rows, hidden)
    )
    wide = hidden // 3
    dy_half = lax.dynamic_slice_in_dim(dy_all.reshape(blocks * rows, width), node * half, half, 1)
    grad_down = left_t(by_token[:, 2 * wide:], dy_half)
    grad_gate = left_t(x_all, by_token[:, :wide])
    grad_up = left_t(x_all, by_token[:, wide:2 * wide])
    return (grad_tokens, grad_gate, grad_up, grad_down)


def solution(mesh):
    in_specs = (
        P(("groups", "cross", "node"), None),
        P(("groups", "cross", "node"), None),
        P(("groups", "cross", "node"), None),
        P(None, ("groups", "node"), "cross"),
        P(None, ("groups", "node"), "cross"),
        P("node", None, "cross"),
        P("node", None, "cross"),
        P("node", "cross", None),
        P(None, "cross"),
        P(None, "cross"),
        P("cross", None),
    )
    out_specs = (
        P(("groups", "cross", "node"), None),
        P(("groups", "node"), "cross"),
        P(("groups", "node"), "cross"),
        P(("groups", "cross"), "node"),
    )
    return jax.shard_map(body, mesh=mesh, in_specs=in_specs, out_specs=out_specs, check_vma=False)
```

```python
import functools

import jax
import jax.numpy as jnp
from jax import lax
from jax.experimental import pallas as pl
from jax.experimental.pallas import tpu as pltpu
from jax.sharding import PartitionSpec as P

CAP = 72
MESH = pl.DeviceIdType.MESH
GATHER_PIECES = 2


def silu_parts(pre_gate, pre_up, grad_hidden):
    sigma = jax.nn.sigmoid(pre_gate)
    active = pre_gate * sigma
    d_gate = grad_hidden * pre_up * sigma * (1.0 + pre_gate * (1.0 - sigma))
    d_up = grad_hidden * active
    return (d_gate, d_up, active * pre_up)


def right_t(left, right):
    return lax.dot_general(
        left, right, (((1,), (1,)), ((), ())), preferred_element_type=jnp.float32
    )


def left_t(left, right):
    return lax.dot_general(
        left, right, (((0,), (0,)), ((), ())), preferred_element_type=jnp.float32
    )


def place(depth):
    cross = lax.axis_index("cross")
    return lax.div(cross, 2), lax.rem(cross, 2), lax.axis_index("node")


def greet(z, y, n, depth):
    barrier = pltpu.get_barrier_semaphore()

    def tell(zz, yy, nn):
        pl.semaphore_signal(
            barrier, inc=1, device_id={"cross": zz * 2 + yy, "node": nn}, device_id_type=MESH
        )

    tell(z, 1 - y, n)
    tell(z, y, 1 - n)

    @pl.when(z < depth - 1)
    def _():
        tell(z + 1, y, n)

    @pl.when(z > 0)
    def _():
        tell(z - 1, y, n)

    count = 2 + (z < depth - 1).astype(jnp.int32) + (z > 0).astype(jnp.int32)
    pl.semaphore_wait(barrier, count)


def gather_kernel(
    depth, dy, ids, x, dy_all, ids_all, xh,
    recv, recv_b, send_r, send_l, send_y, send_b, x_send, x_recv, local_sem,
):
    z, y, n = place(depth)
    rows = dy.shape[0] // GATHER_PIECES
    half = xh.shape[-1]
    pieces = GATHER_PIECES + 1
    greet(z, y, n, depth)

    def slot(c, core, h):
        if h < GATHER_PIECES:
            return dy_all.at[c, core, pl.ds(h * rows, rows)]
        return ids_all.at[c, core]

    def own(h):
        if h < GATHER_PIECES:
            return dy.at[pl.ds(h * rows, rows)]
        return ids

    def copy(src, c, h, send_sem, recv_sem, zz, yy, nn):
        return pltpu.make_async_remote_copy(
            src_ref=src,
            dst_ref=slot(c, n, h),
            send_sem=send_sem,
            recv_sem=recv_sem.at[c, h],
            device_id={"cross": zz * 2 + yy, "node": nn},
            device_id_type=MESH,
        )

    def right(src, zb, h):
        return copy(src, zb * 2 + y, h, send_r.at[zb, h], recv, z + 1, y, n)

    def left(src, zb, h):
        return copy(src, zb * 2 + y, h, send_l.at[zb, h], recv, z - 1, y, n)

    def across(src, zb, h):
        return copy(src, zb * 2 + y, h, send_y.at[zb, h], recv, z, 1 - y, n)

    def sibling(src, c, h):
        return copy(src, c, h, send_b.at[c, h], recv_b, z, y, 1 - n)

    def arrived(c, h):
        pltpu.make_async_remote_copy(
            src_ref=slot(c, n, h), dst_ref=slot(c, n, h), send_sem=send_b.at[c, h],
            recv_sem=recv.at[c, h], device_id={"cross": z * 2 + y, "node": 1 - n},
            device_id_type=MESH,
        ).wait_recv()

    def arrived_b(c, h):
        pltpu.make_async_remote_copy(
            src_ref=slot(c, 1 - n, h), dst_ref=slot(c, 1 - n, h), send_sem=send_b.at[c, h],
            recv_sem=recv_b.at[c, h], device_id={"cross": z * 2 + y, "node": 1 - n},
            device_id_type=MESH,
        ).wait_recv()

    def mine(src, zb, h, act):
        @pl.when((z < depth - 1) & (zb <= z))
        def _():
            act(right(src, zb, h))

        @pl.when((z > 0) & (zb >= z))
        def _():
            act(left(src, zb, h))

        act(across(src, zb, h))
        act(sibling(src, zb * 2 + y, h))

    def start(d):
        d.start()

    def done(d):
        d.wait_send()

    def walk(s, act):
        if s == 0:
            act(z)
        else:
            @pl.when(z - s >= 0)
            def _():
                act(z - s)

            @pl.when(z + s < depth)
            def _():
                act(z + s)

    order = [GATHER_PIECES] + list(range(GATHER_PIECES))
    for h in order:
        mine(own(h), z, h, start)
    keep = pl.multiple_of(n * half, 128)
    give = pl.multiple_of((1 - n) * half, 128)
    x_out = pltpu.make_async_remote_copy(
        src_ref=x.at[:, pl.ds(give, half)], dst_ref=xh.at[n], send_sem=x_send, recv_sem=x_recv,
        device_id={"cross": z * 2 + y, "node": 1 - n}, device_id_type=MESH,
    )
    x_out.start()
    locals_ = [
        pltpu.make_async_copy(dy, dy_all.at[z * 2 + y, n], local_sem.at[0]),
        pltpu.make_async_copy(ids, ids_all.at[z * 2 + y, n], local_sem.at[1]),
        pltpu.make_async_copy(x.at[:, pl.ds(keep, half)], xh.at[n], local_sem.at[2]),
    ]
    for d in locals_:
        d.start()

    def down(h):
        def act(zb):
            arrived(zb * 2 + y, h)
            mine(slot(zb * 2 + y, n, h), zb, h, start)
        return act

    def over(h):
        def act(zb):
            c = zb * 2 + 1 - y
            arrived(c, h)
            sibling(slot(c, n, h), c, h).start()
        return act

    for s in range(1, depth + 1):
        for h in order:
            if s < depth:
                walk(s, down(h))
            walk(s - 1, over(h))

    for d in locals_:
        d.wait()
    x_out.wait_send()
    pltpu.make_async_remote_copy(
        src_ref=xh.at[1 - n], dst_ref=xh.at[1 - n], send_sem=x_send, recv_sem=x_recv,
        device_id={"cross": z * 2 + y, "node": 1 - n}, device_id_type=MESH,
    ).wait_recv()
    for h in range(pieces):
        for zb in range(depth):
            mine(slot(zb * 2 + y, n, h), zb, h, done)
            c = zb * 2 + 1 - y
            sibling(slot(c, n, h), c, h).wait_send()
            arrived_b(zb * 2, h)
            arrived_b(zb * 2 + 1, h)


def gather(dy, ids, x, count):
    depth = count // 2
    rows, width = dy.shape
    pieces = GATHER_PIECES + 1
    dma = pltpu.SemaphoreType.DMA
    hbm = pl.BlockSpec(memory_space=pl.ANY)
    return pl.pallas_call(
        functools.partial(gather_kernel, depth),
        out_shape=(
            jax.ShapeDtypeStruct((count, 2, rows, width), dy.dtype),
            jax.ShapeDtypeStruct((count, 2) + ids.shape, ids.dtype),
            jax.ShapeDtypeStruct((2, rows, width // 2), x.dtype),
        ),
        in_specs=[hbm] * 3,
        out_specs=(hbm,) * 3,
        scratch_shapes=[
            dma((count, pieces)),
            dma((count, pieces)),
            dma((depth, pieces)),
            dma((depth, pieces)),
            dma((depth, pieces)),
            dma((count, pieces)),
            dma,
            dma,
            dma((3,)),
        ],
        compiler_params=pltpu.CompilerParams(collective_id=0, has_side_effects=True),
        name="gather_rows",
    )(dy, ids, x)


def line_pairs(depth, step, s):
    pairs = []
    for z in range(depth):
        if 0 <= z + step * s < depth:
            pairs += [(z * 2 + y, (z + step) * 2 + y) for y in range(2)]
    return pairs


def across_pairs(depth, step, s):
    return [
        (z * 2 + y, z * 2 + 1 - y)
        for z in range(depth)
        if 0 <= z + step * s < depth
        for y in range(2)
    ]


def gather_step(x, count, until, came):
    depth = count // 2
    for step in (1, -1):
        start = 1 + max([s for (k, s) in came if k == step], default=0)
        block = came[step, start - 1][0] if start > 1 else x
        for s in range(start, min(until + 1, depth)):
            pairs = [
                (z * 2 + y, (z + step) * 2 + y)
                for z in range(depth)
                if 0 <= z + step < depth and 0 <= z - step * (s - 1) < depth
                for y in range(2)
            ]
            block = lax.ppermute(block, "cross", pairs)
            came[step, s] = (block, None)
    return came


def held_until(came, s, *values):
    right, left, *values = lax.optimization_barrier(
        (came[1, s][0], came[-1, s][0]) + values
    )
    depth = lax.axis_size("cross") // 2
    for step, block in ((1, right), (-1, left)):
        over = lax.ppermute(block, "cross", across_pairs(depth, -step, s))
        came[step, s] = (block, over)
    return values


def by_distance(x, first, came, count):
    depth = count // 2
    out = [x, first]
    for s in range(1, depth):
        for j in range(2):
            out.append(came[-1, s][j] + came[1, depth - s][j])
    return jnp.concatenate(out, axis=0)


def reduce_rows(part, count):
    depth = count // 2
    z, y = lax.div(lax.axis_index("cross"), 2), lax.rem(lax.axis_index("cross"), 2)
    f32 = jnp.float32

    def pick(d, column):
        return lax.dynamic_slice(
            part, (d, column, 0, 0), (1, 1) + part.shape[2:]
        ).reshape(part.shape[2:])

    def base(step, s):
        d = jnp.clip(z + step * s, 0, depth - 1)
        got = lax.ppermute(pick(d, 1 - y), "cross", across_pairs(depth, step, s))
        return pick(d, y).astype(f32) + got.astype(f32)

    moving = {1: None, -1: None}
    for s in range(depth - 1, 0, -1):
        for step in (1, -1):
            total = base(step, s)
            if moving[step] is not None:
                total = total + moving[step].astype(f32)
            moving[step] = lax.ppermute(
                total.astype(part.dtype), "cross", line_pairs(depth, step, s)
            )
    total = base(1, 0) + moving[1].astype(f32) + moving[-1].astype(f32)
    total = total.astype(part.dtype)
    other = lax.ppermute(total, "node", [(0, 1), (1, 0)])
    first = jnp.where(lax.axis_index("node") == 0, total, other)
    second = jnp.where(lax.axis_index("node") == 0, other, total)
    return jnp.stack([first, second])


def slots_of(ids, expert):
    named = (ids == expert).astype(jnp.bfloat16)
    tokens = ids.shape[1]
    upper = (
        jnp.arange(tokens)[:, None] <= jnp.arange(tokens)[None, :]
    ).astype(jnp.bfloat16)
    rank = lax.dot_general(
        named, upper, (((1,), (0,)), ((), ())), preferred_element_type=jnp.float32
    ).astype(jnp.int32) - 1
    slot = jnp.where(ids == expert, rank, -1)
    return (slot[:, None, :] == jnp.arange(CAP, dtype=jnp.int32)[None, :, None]).astype(
        jnp.bfloat16
    )


def body(
    tokens, grad_out, expert_ids, routed_pre, shared_pre, w_gate, w_up, w_down, s_gate, s_up, s_down
):
    count = lax.axis_size("cross")
    node = lax.axis_index("node")
    cross = lax.axis_index("cross")
    rows, width = tokens.shape
    half = width // 2
    ids_tile = jnp.broadcast_to(expert_ids[:, 0][None, :], (8, rows))
    dy_all, ids_all, x_half = gather(grad_out, ids_tile, tokens, count)
    x_block = x_half.reshape(2 * rows, half)
    depth = count // 2
    across = lax.ppermute(x_block, "cross", across_pairs(depth, 1, 0))
    came = gather_step(x_block, count, 1, {})
    blocks = 2 * count
    dy_all = dy_all.reshape(blocks, rows, width)
    ids = ids_all[:, :, 0, :].reshape(blocks, rows)
    to_slots = slots_of(ids, node)
    to_slots_b = slots_of(ids, 1 - node)
    dy_rows = (
        jnp.einsum("bst,btd->bsd", to_slots, dy_all, preferred_element_type=jnp.float32)
        .astype(jnp.bfloat16)
        .reshape(blocks * CAP, width)
    )
    sh_gate, sh_up, shared_act = silu_parts(
        shared_pre[0].astype(jnp.float32),
        shared_pre[1].astype(jnp.float32),
        right_t(dy_rows, s_down),
    )
    sh_gate = sh_gate.astype(jnp.bfloat16)
    sh_up = sh_up.astype(jnp.bfloat16)
    shared_act = shared_act.astype(jnp.bfloat16)
    mine = jnp.concatenate([sh_gate, sh_up, shared_act], axis=1)
    other = lax.ppermute(mine, "node", [(0, 1), (1, 0)])
    d_gate, d_up, _ = silu_parts(
        routed_pre[0].astype(jnp.float32),
        routed_pre[1].astype(jnp.float32),
        right_t(dy_rows, w_down[0]),
    )
    d_gate = d_gate.astype(jnp.bfloat16)
    d_up = d_up.astype(jnp.bfloat16)
    d_gate, d_up = held_until(came, 1, d_gate, d_up)
    gather_step(x_block, count, 2, came)
    partial_in = right_t(d_gate, w_gate[0]) + right_t(d_up, w_up[0])
    (partial_in,) = held_until(came, 2, partial_in)
    gather_step(x_block, count, depth - 1, came)
    partial_in = (partial_in + right_t(sh_gate, s_gate) + right_t(sh_up, s_up)).astype(
        jnp.bfloat16
    )
    right, left, partial_in = lax.optimization_barrier(
        (came[1, 1][1], came[-1, 1][1], partial_in)
    )
    came[1, 1] = (came[1, 1][0], right)
    came[-1, 1] = (came[-1, 1][0], left)
    (partial_in,) = held_until(came, 3, partial_in)
    for s in range(4, depth):
        held_until(came, s)
    x_all = by_distance(x_block, across, came, count)
    returned = reduce_rows(partial_in.reshape(count // 2, 2, 2 * CAP, width), count)

    own_ids = expert_ids[:, 0].reshape(1, rows)
    picks = jnp.stack([slots_of(own_ids, e)[0] for e in range(2)])
    picks = jnp.where(
        (jnp.arange(2) == node)[None, :, None, None], picks[:, None], jnp.zeros((), jnp.bfloat16)
    ).reshape(4 * CAP, rows)
    grad_tokens = left_t(picks, returned.reshape(4 * CAP, width)).astype(jnp.bfloat16)

    hidden = mine.shape[1]

    def to_tokens(one_hot, values):
        return jnp.einsum(
            "bst,bsf->btf", one_hot, values.reshape(blocks, CAP, hidden),
            preferred_element_type=jnp.float32,
        )

    by_token = (
        (to_tokens(to_slots, mine) + to_tokens(to_slots_b, other))
        .astype(jnp.bfloat16)
        .reshape(blocks * rows, hidden)
    )
    wide = hidden // 3
    dy_half = lax.dynamic_slice_in_dim(dy_all.reshape(blocks * rows, width), node * half, half, 1)
    grad_down = left_t(by_token[:, 2 * wide:], dy_half)
    z, y = lax.div(cross, 2), lax.rem(cross, 2)
    far = jnp.arange(count, dtype=jnp.int32)
    order = lax.rem(z + far // 2, count // 2) * 2 + jnp.where(far % 2 == 0, y, 1 - y)
    near = jnp.take(
        by_token[:, :2 * wide].reshape(count, 2 * rows, 2 * wide), order, axis=0,
        mode="clip",
    ).reshape(blocks * rows, 2 * wide)
    grad_gate = left_t(x_all, near[:, :wide])
    grad_up = left_t(x_all, near[:, wide:])
    return (grad_tokens, grad_gate, grad_up, grad_down)


def solution(mesh):
    in_specs = (
        P(("groups", "cross", "node"), None),
        P(("groups", "cross", "node"), None),
        P(("groups", "cross", "node"), None),
        P(None, ("groups", "node"), "cross"),
        P(None, ("groups", "node"), "cross"),
        P("node", None, "cross"),
        P("node", None, "cross"),
        P("node", "cross", None),
        P(None, "cross"),
        P(None, "cross"),
        P("cross", None),
    )
    out_specs = (
        P(("groups", "cross", "node"), None),
        P(("groups", "node"), "cross"),
        P(("groups", "node"), "cross"),
        P(("groups", "cross"), "node"),
    )
    return jax.shard_map(body, mesh=mesh, in_specs=in_specs, out_specs=out_specs, check_vma=False)
```

```python
import functools

import jax
import jax.numpy as jnp
from jax import lax
from jax.experimental import pallas as pl
from jax.experimental.pallas import tpu as pltpu
from jax.sharding import PartitionSpec as P

CAP = 72
MESH = pl.DeviceIdType.MESH
GATHER_PIECES = 2
REDUCE_PIECES = 3


def silu_parts(pre_gate, pre_up, grad_hidden):
    sigma = jax.nn.sigmoid(pre_gate)
    active = pre_gate * sigma
    d_gate = grad_hidden * pre_up * sigma * (1.0 + pre_gate * (1.0 - sigma))
    d_up = grad_hidden * active
    return (d_gate, d_up, active * pre_up)


def right_t(left, right):
    return lax.dot_general(
        left, right, (((1,), (1,)), ((), ())), preferred_element_type=jnp.float32
    )


def left_t(left, right):
    return lax.dot_general(
        left, right, (((0,), (0,)), ((), ())), preferred_element_type=jnp.float32
    )


def place(depth):
    cross = lax.axis_index("cross")
    return lax.div(cross, 2), lax.rem(cross, 2), lax.axis_index("node")


def greet(z, y, n, depth):
    barrier = pltpu.get_barrier_semaphore()

    def tell(zz, yy, nn):
        pl.semaphore_signal(
            barrier, inc=1, device_id={"cross": zz * 2 + yy, "node": nn}, device_id_type=MESH
        )

    tell(z, 1 - y, n)
    tell(z, y, 1 - n)

    @pl.when(z < depth - 1)
    def _():
        tell(z + 1, y, n)

    @pl.when(z > 0)
    def _():
        tell(z - 1, y, n)

    count = 2 + (z < depth - 1).astype(jnp.int32) + (z > 0).astype(jnp.int32)
    pl.semaphore_wait(barrier, count)


def gather_kernel(
    depth, dy, ids, x, dy_all, ids_all, xh,
    recv, recv_b, send_r, send_l, send_y, send_b, x_send, x_recv, local_sem,
):
    z, y, n = place(depth)
    rows = dy.shape[0] // GATHER_PIECES
    half = xh.shape[-1]
    pieces = GATHER_PIECES + 1
    greet(z, y, n, depth)

    def slot(c, core, h):
        if h < GATHER_PIECES:
            return dy_all.at[c, core, pl.ds(h * rows, rows)]
        return ids_all.at[c, core]

    def own(h):
        if h < GATHER_PIECES:
            return dy.at[pl.ds(h * rows, rows)]
        return ids

    def copy(src, c, h, send_sem, recv_sem, zz, yy, nn):
        return pltpu.make_async_remote_copy(
            src_ref=src,
            dst_ref=slot(c, n, h),
            send_sem=send_sem,
            recv_sem=recv_sem.at[c, h],
            device_id={"cross": zz * 2 + yy, "node": nn},
            device_id_type=MESH,
        )

    def right(src, zb, h):
        return copy(src, zb * 2 + y, h, send_r.at[zb, h], recv, z + 1, y, n)

    def left(src, zb, h):
        return copy(src, zb * 2 + y, h, send_l.at[zb, h], recv, z - 1, y, n)

    def across(src, zb, h):
        return copy(src, zb * 2 + y, h, send_y.at[zb, h], recv, z, 1 - y, n)

    def sibling(src, c, h):
        return copy(src, c, h, send_b.at[c, h], recv_b, z, y, 1 - n)

    def arrived(c, h):
        pltpu.make_async_remote_copy(
            src_ref=slot(c, n, h), dst_ref=slot(c, n, h), send_sem=send_b.at[c, h],
            recv_sem=recv.at[c, h], device_id={"cross": z * 2 + y, "node": 1 - n},
            device_id_type=MESH,
        ).wait_recv()

    def arrived_b(c, h):
        pltpu.make_async_remote_copy(
            src_ref=slot(c, 1 - n, h), dst_ref=slot(c, 1 - n, h), send_sem=send_b.at[c, h],
            recv_sem=recv_b.at[c, h], device_id={"cross": z * 2 + y, "node": 1 - n},
            device_id_type=MESH,
        ).wait_recv()

    def mine(src, zb, h, act):
        @pl.when((z < depth - 1) & (zb <= z))
        def _():
            act(right(src, zb, h))

        @pl.when((z > 0) & (zb >= z))
        def _():
            act(left(src, zb, h))

        act(across(src, zb, h))
        act(sibling(src, zb * 2 + y, h))

    def start(d):
        d.start()

    def done(d):
        d.wait_send()

    def walk(s, act):
        if s == 0:
            act(z)
        else:
            @pl.when(z - s >= 0)
            def _():
                act(z - s)

            @pl.when(z + s < depth)
            def _():
                act(z + s)

    order = [GATHER_PIECES] + list(range(GATHER_PIECES))
    for h in order:
        mine(own(h), z, h, start)
    keep = pl.multiple_of(n * half, 128)
    give = pl.multiple_of((1 - n) * half, 128)
    x_out = pltpu.make_async_remote_copy(
        src_ref=x.at[:, pl.ds(give, half)], dst_ref=xh.at[n], send_sem=x_send, recv_sem=x_recv,
        device_id={"cross": z * 2 + y, "node": 1 - n}, device_id_type=MESH,
    )
    x_out.start()
    locals_ = [
        pltpu.make_async_copy(dy, dy_all.at[z * 2 + y, n], local_sem.at[0]),
        pltpu.make_async_copy(ids, ids_all.at[z * 2 + y, n], local_sem.at[1]),
        pltpu.make_async_copy(x.at[:, pl.ds(keep, half)], xh.at[n], local_sem.at[2]),
    ]
    for d in locals_:
        d.start()

    def down(h):
        def act(zb):
            arrived(zb * 2 + y, h)
            mine(slot(zb * 2 + y, n, h), zb, h, start)
        return act

    def over(h):
        def act(zb):
            c = zb * 2 + 1 - y
            arrived(c, h)
            sibling(slot(c, n, h), c, h).start()
        return act

    for s in range(1, depth + 1):
        for h in order:
            if s < depth:
                walk(s, down(h))
            walk(s - 1, over(h))

    for d in locals_:
        d.wait()
    x_out.wait_send()
    pltpu.make_async_remote_copy(
        src_ref=xh.at[1 - n], dst_ref=xh.at[1 - n], send_sem=x_send, recv_sem=x_recv,
        device_id={"cross": z * 2 + y, "node": 1 - n}, device_id_type=MESH,
    ).wait_recv()
    for h in range(pieces):
        for zb in range(depth):
            mine(slot(zb * 2 + y, n, h), zb, h, done)
            c = zb * 2 + 1 - y
            sibling(slot(c, n, h), c, h).wait_send()
            arrived_b(zb * 2, h)
            arrived_b(zb * 2 + 1, h)


def gather(dy, ids, x, count):
    depth = count // 2
    rows, width = dy.shape
    pieces = GATHER_PIECES + 1
    dma = pltpu.SemaphoreType.DMA
    hbm = pl.BlockSpec(memory_space=pl.ANY)
    return pl.pallas_call(
        functools.partial(gather_kernel, depth),
        out_shape=(
            jax.ShapeDtypeStruct((count, 2, rows, width), dy.dtype),
            jax.ShapeDtypeStruct((count, 2) + ids.shape, ids.dtype),
            jax.ShapeDtypeStruct((2, rows, width // 2), x.dtype),
        ),
        in_specs=[hbm] * 3,
        out_specs=(hbm,) * 3,
        scratch_shapes=[
            dma((count, pieces)),
            dma((count, pieces)),
            dma((depth, pieces)),
            dma((depth, pieces)),
            dma((depth, pieces)),
            dma((count, pieces)),
            dma,
            dma,
            dma((3,)),
        ],
        compiler_params=pltpu.CompilerParams(collective_id=0, has_side_effects=True),
        name="gather_rows",
    )(dy, ids, x)


def reduce_kernel(
    depth, part, out, y_buf, r_buf, l_buf, held,
    y_send, y_recv, r_send, r_recv, l_send, l_recv, b_send, b_recv,
):
    z, y, n = place(depth)
    rows = part.shape[2] // REDUCE_PIECES
    greet(z, y, n, depth)

    def at(ref, d, h):
        return ref.at[d, pl.ds(h * rows, rows)]

    def copy(src, dst, send_sem, recv_sem, zz, yy, nn):
        return pltpu.make_async_remote_copy(
            src_ref=src, dst_ref=dst, send_sem=send_sem, recv_sem=recv_sem,
            device_id={"cross": zz * 2 + yy, "node": nn}, device_id_type=MESH,
        )

    def across(d, h):
        return copy(
            part.at[d, 1 - y, pl.ds(h * rows, rows)], at(y_buf, d, h),
            y_send.at[d, h], y_recv.at[d, h], z, 1 - y, n,
        )

    def right(d, h):
        return copy(
            at(held, d, h), at(r_buf, d, h), r_send.at[d, h], r_recv.at[d, h], z + 1, y, n
        )

    def left(d, h):
        return copy(
            at(held, d, h), at(l_buf, d, h), l_send.at[d, h], l_recv.at[d, h], z - 1, y, n
        )

    def sibling(h):
        return copy(
            at(out, n, h), at(out, n, h), b_send.at[h], b_recv.at[h], z, y, 1 - n
        )

    def walk(s, act):
        if s == 0:
            act(z)
        else:
            @pl.when(z + s < depth)
            def _():
                act(z + s)

            @pl.when(z - s >= 0)
            def _():
                act(z - s)

    def begin(s):
        for h in range(REDUCE_PIECES):
            walk(s, lambda d, h=h: across(d, h).start())

    def base(d, h):
        across(d, h).wait_recv()
        return part[d, y, pl.ds(h * rows, rows)].astype(jnp.float32) + y_buf[
            d, pl.ds(h * rows, rows)
        ].astype(jnp.float32)

    begin(depth - 1)
    for s in range(depth - 1, 0, -1):
        begin(s - 1)
        for h in range(REDUCE_PIECES):
            span = pl.ds(h * rows, rows)

            @pl.when(z + s < depth)
            def _():
                d = z + s
                value = base(d, h)
                if s == depth - 1:
                    held[d, span] = value.astype(held.dtype)
                else:
                    @pl.when(z == 0)
                    def _():
                        held[d, span] = value.astype(held.dtype)

                    @pl.when(z > 0)
                    def _():
                        right(d, h).wait_recv()
                        total = value + r_buf[d, span].astype(jnp.float32)
                        held[d, span] = total.astype(held.dtype)

                right(d, h).start()

            @pl.when(z - s >= 0)
            def _():
                d = z - s
                value = base(d, h)
                if s == depth - 1:
                    held[d, span] = value.astype(held.dtype)
                else:
                    @pl.when(z == depth - 1)
                    def _():
                        held[d, span] = value.astype(held.dtype)

                    @pl.when(z < depth - 1)
                    def _():
                        left(d, h).wait_recv()
                        total = value + l_buf[d, span].astype(jnp.float32)
                        held[d, span] = total.astype(held.dtype)

                left(d, h).start()

    for h in range(REDUCE_PIECES):
        span = pl.ds(h * rows, rows)
        value = base(z, h)

        @pl.when(z == 0)
        def _():
            left(z, h).wait_recv()
            out[n, span] = (value + l_buf[z, span].astype(jnp.float32)).astype(out.dtype)

        @pl.when(z == depth - 1)
        def _():
            right(z, h).wait_recv()
            out[n, span] = (value + r_buf[z, span].astype(jnp.float32)).astype(out.dtype)

        @pl.when((z > 0) & (z < depth - 1))
        def _():
            left(z, h).wait_recv()
            right(z, h).wait_recv()
            total = (
                value + l_buf[z, span].astype(jnp.float32) + r_buf[z, span].astype(jnp.float32)
            )
            out[n, span] = total.astype(out.dtype)

        sibling(h).start()

    for h in range(REDUCE_PIECES):
        for d in range(depth):
            across(d, h).wait_send()

            @pl.when(z < d)
            def _():
                right(d, h).wait_send()

            @pl.when(z > d)
            def _():
                left(d, h).wait_send()

        sibling(h).wait_send()
        copy(
            at(out, 1 - n, h), at(out, 1 - n, h), b_send.at[h], b_recv.at[h], z, y, 1 - n
        ).wait_recv()


def reduce_rows(part, count):
    depth = count // 2
    _, _, rows, width = part.shape
    dma = pltpu.SemaphoreType.DMA
    vmem = pl.BlockSpec(memory_space=pltpu.VMEM)
    pair = (depth, REDUCE_PIECES)
    block = pltpu.VMEM((depth, rows, width), part.dtype)
    return pl.pallas_call(
        functools.partial(reduce_kernel, depth),
        out_shape=jax.ShapeDtypeStruct((2, rows, width), part.dtype),
        in_specs=[vmem],
        out_specs=vmem,
        scratch_shapes=[block] * 4
        + [dma(pair)] * 6
        + [dma((REDUCE_PIECES,))] * 2,
        compiler_params=pltpu.CompilerParams(
            collective_id=1, has_side_effects=True, vmem_limit_bytes=56 * 1024 * 1024
        ),
        name="reduce_rows",
    )(part)


def slots_of(ids, expert):
    named = (ids == expert).astype(jnp.bfloat16)
    tokens = ids.shape[1]
    upper = (
        jnp.arange(tokens)[:, None] <= jnp.arange(tokens)[None, :]
    ).astype(jnp.bfloat16)
    rank = lax.dot_general(
        named, upper, (((1,), (0,)), ((), ())), preferred_element_type=jnp.float32
    ).astype(jnp.int32) - 1
    slot = jnp.where(ids == expert, rank, -1)
    return (slot[:, None, :] == jnp.arange(CAP, dtype=jnp.int32)[None, :, None]).astype(
        jnp.bfloat16
    )


def body(
    tokens, grad_out, expert_ids, routed_pre, shared_pre, w_gate, w_up, w_down, s_gate, s_up, s_down
):
    count = lax.axis_size("cross")
    node = lax.axis_index("node")
    cross = lax.axis_index("cross")
    rows, width = tokens.shape
    half = width // 2
    ids_tile = jnp.broadcast_to(expert_ids[:, 0][None, :], (8, rows))
    dy_all, ids_all, x_half = gather(grad_out, ids_tile, tokens, count)
    x_all = lax.all_gather(x_half.reshape(2 * rows, half), "cross", axis=0, tiled=True)
    blocks = 2 * count
    dy_all = dy_all.reshape(blocks, rows, width)
    ids = ids_all[:, :, 0, :].reshape(blocks, rows)
    to_slots = slots_of(ids, node)
    to_slots_b = slots_of(ids, 1 - node)
    dy_rows = (
        jnp.einsum("bst,btd->bsd", to_slots, dy_all, preferred_element_type=jnp.float32)
        .astype(jnp.bfloat16)
        .reshape(blocks * CAP, width)
    )
    sh_gate, sh_up, shared_act = silu_parts(
        shared_pre[0].astype(jnp.float32),
        shared_pre[1].astype(jnp.float32),
        right_t(dy_rows, s_down),
    )
    sh_gate = sh_gate.astype(jnp.bfloat16)
    sh_up = sh_up.astype(jnp.bfloat16)
    shared_act = shared_act.astype(jnp.bfloat16)
    mine = jnp.concatenate([sh_gate, sh_up, shared_act], axis=1)
    other = lax.ppermute(mine, "node", [(0, 1), (1, 0)])
    d_gate, d_up, _ = silu_parts(
        routed_pre[0].astype(jnp.float32),
        routed_pre[1].astype(jnp.float32),
        right_t(dy_rows, w_down[0]),
    )
    d_gate = d_gate.astype(jnp.bfloat16)
    d_up = d_up.astype(jnp.bfloat16)
    partial_in = (
        right_t(d_gate, w_gate[0])
        + right_t(d_up, w_up[0])
        + right_t(sh_gate, s_gate)
        + right_t(sh_up, s_up)
    ).astype(jnp.bfloat16)
    hidden = mine.shape[1]

    def to_tokens(one_hot, values):
        return jnp.einsum(
            "bst,bsf->btf", one_hot, values.reshape(blocks, CAP, hidden),
            preferred_element_type=jnp.float32,
        )

    by_token = (
        (to_tokens(to_slots, mine) + to_tokens(to_slots_b, other))
        .astype(jnp.bfloat16)
        .reshape(blocks * rows, hidden)
    )
    wide = hidden // 3
    dy_half = lax.dynamic_slice_in_dim(dy_all.reshape(blocks * rows, width), node * half, half, 1)
    grad_down = left_t(by_token[:, 2 * wide:], dy_half)
    partial_in, by_token, grad_down = lax.optimization_barrier((partial_in, by_token, grad_down))
    returned = reduce_rows(partial_in.reshape(count // 2, 2, 2 * CAP, width), count)

    own_ids = expert_ids[:, 0].reshape(1, rows)
    picks = jnp.stack([slots_of(own_ids, e)[0] for e in range(2)])
    picks = jnp.where(
        (jnp.arange(2) == node)[None, :, None, None], picks[:, None], jnp.zeros((), jnp.bfloat16)
    ).reshape(4 * CAP, rows)
    grad_tokens = left_t(picks, returned.reshape(4 * CAP, width)).astype(jnp.bfloat16)
    grad_gate = left_t(x_all, by_token[:, :wide])
    grad_up = left_t(x_all, by_token[:, wide:2 * wide])
    return (grad_tokens, grad_gate, grad_up, grad_down)


def solution(mesh):
    in_specs = (
        P(("groups", "cross", "node"), None),
        P(("groups", "cross", "node"), None),
        P(("groups", "cross", "node"), None),
        P(None, ("groups", "node"), "cross"),
        P(None, ("groups", "node"), "cross"),
        P("node", None, "cross"),
        P("node", None, "cross"),
        P("node", "cross", None),
        P(None, "cross"),
        P(None, "cross"),
        P("cross", None),
    )
    out_specs = (
        P(("groups", "cross", "node"), None),
        P(("groups", "node"), "cross"),
        P(("groups", "node"), "cross"),
        P(("groups", "cross"), "node"),
    )
    return jax.shard_map(body, mesh=mesh, in_specs=in_specs, out_specs=out_specs, check_vma=False)
```
